32 devices in a mesh: groups: 2 (over y), dp: 8 (over z, x), tensor: 2 (over core).
Axes of the slice: x: 2, y: 2, z: 4, core: 2. Of those that a mesh axis runs over, the one named last changes fastest.
Arguments:
- tokens: bfloat16 [6144, 5120], P(('groups', 'dp'), 'tensor'), parts along dimension 0, may hold values from -6 to 6
- expert_ids: int32 [6144, 6], P(('groups', 'dp')), parts along dimension 0, may hold values from 0 to 159, as said below
- combine: float32 [6144, 6], P(('groups', 'dp')), parts along dimension 0, may hold values from 0.1 to 1
- row_list: int32 [6144], P(('groups', 'dp')), parts along dimension 0, may hold values from -1 to 383, as said below
- gate_q: bfloat16 [5120, 768], P('dp', 'tensor'), may hold values from -0.078125 to 0.078125
- gate_scale: float32 [5120, 6], P('dp', 'tensor'), may hold values from 0.3 to 3
- up_q: bfloat16 [5120, 768], P('dp', 'tensor'), may hold values from -0.078125 to 0.078125
- up_scale: float32 [5120, 6], P('dp', 'tensor'), may hold values from 0.3 to 3
- down_q: bfloat16 [768, 5120], P('tensor', 'dp'), may hold values from -0.21875 to 0.21875
- down_scale: float32 [6, 5120], P('tensor', 'dp'), may hold values from 0.3 to 3
Outputs:
- expert_output: bfloat16 [6144, 5120], P(('groups', 'dp'), 'tensor'), parts along dimension 0
The draws below stay inside these ranges and needn't reach their ends.
There are 2 independent parts, one for each index of `groups`. The reference program is written for one: setup_inputs(seed, part) draws one part's arguments, and reference() takes and returns one part's arrays. A program takes and returns all parts, laid end to end along the dimension named above; an argument that names none is the same for every part. Nothing has to cross between parts.
Inputs may be any that keep to these rules, and one draw needn't show every extreme that they name: `expert_ids`: each row holds 6 different expert numbers; expert 0 is the expert whose weights are given. `row_list`: each index of dp has 384 entries: in ascending order the local rows (0 to 383 in that index's block of tokens) whose expert_ids name expert 0, then -1. The last index of dp lists all 384 of its rows.
All inputs are finite; a program needn't handle non-finite values.
Results may differ from the reference program's by a relative error of at most 0.02.
Values may be sent and summed in bfloat16 or wider, within the bound.
A program may use at most 128 MiB of HBM per device.

```python
import math
import jax
import jax.numpy as jnp
from jax import lax

D = 5120
FW = 768
EXPERTS = 160
TOPK = 6
TILE = 128
TOK_DEV = 384
TOKENS = 3072
N_TENSOR = 2


def routing(key):
    first, second, third, fourth = jax.random.split(key, 4)
    owner_index = jnp.arange(TOKENS, dtype=jnp.int32) // TOK_DEV
    last_owner = max(TOKENS // TOK_DEV - 1, 1)
    threshold = 250 + 750 * owner_index // last_owner
    routed = jax.random.randint(first, (TOKENS,), 0, 1000) < threshold
    base_id = jax.random.randint(second, (TOKENS, 1), 0, EXPERTS - 1)
    stride = jax.random.randint(third, (TOKENS, 1), 1, 27)
    slots = jnp.arange(TOPK, dtype=jnp.int32)[None, :]
    choices_made = 1 + (base_id + slots * stride) % (EXPERTS - 1)
    chosen_slot = jax.random.randint(fourth, (TOKENS, 1), 0, TOPK)
    chosen = jnp.where(routed[:, None] & (slots == chosen_slot), 0, choices_made)
    return (chosen.astype(jnp.int32), routed)


def draw_expert_ids(key, part):
    chosen, routed = routing(key)
    return chosen


def draw_row_list(key, part):
    chosen, routed = routing(key)
    flags = routed.reshape(TOKENS // TOK_DEV, TOK_DEV).astype(jnp.int32)
    local_rows = jnp.arange(TOK_DEV, dtype=jnp.int32)[None, :]
    order_key = (1 - flags) * TOK_DEV + local_rows
    ordering = jnp.argsort(order_key, axis=1, stable=True).astype(jnp.int32)
    sorted_flags = jnp.take_along_axis(flags, ordering, axis=1)
    listed = jnp.where(sorted_flags == 1, ordering, -1)
    return listed.reshape(TOKENS).astype(jnp.int32)


def steps_of(own_key, extent, cuts, least, high):
    loudness, own = 1.0, jax.random.fold_in(own_key, 6)
    for position, blocks in cuts:
        draws = jnp.exp(jax.random.uniform(jax.random.fold_in(own, position), (blocks,), jnp.float32, least / len(cuts), high / len(cuts)))
        loudness = loudness * jnp.repeat(draws, extent[position] // blocks).reshape([-1 if axis == position else 1 for axis in range(len(extent))])
    return loudness


def noise(rng, shape, deviation, bound, pieces=(), held_as=jnp.bfloat16):
    gain = steps_of(rng, shape, pieces, -0.22, 0.18) if pieces else 1.0
    entries = jax.random.normal(rng, shape, jnp.float32) * deviation * gain
    return jnp.minimum(jnp.maximum(entries, -bound), bound).astype(held_as)


def setup_inputs(seed: int = 0, part: int = 0) -> dict:
    streams_of = jax.random.split(jax.random.key(seed), 11)
    own_keys = jax.random.split(jax.random.fold_in(streams_of[10], part), 11)
    return {
        "tokens": noise(own_keys[0], (TOKENS, D), 1.0, 6.0, ((0, 8), (1, 2))),
        "expert_ids": draw_expert_ids(jax.random.fold_in(jax.random.fold_in(streams_of[10], part), 71), part),
        "combine": jnp.clip(jnp.exp(math.log(1.0) - 2.3025851 * jax.random.uniform(own_keys[2], (TOKENS, TOPK), jnp.float32) ** steps_of(own_keys[2], (TOKENS, TOPK), ((0, 8),), -0.2, 0.2)), 0.1, 1.0),
        "row_list": draw_row_list(jax.random.fold_in(jax.random.fold_in(streams_of[10], part), 71), part),
        "gate_q": noise(streams_of[4], (D, FW), D ** -0.5, 0.078125, ((0, 8), (1, 2))),
        "gate_scale": jnp.clip(jnp.exp(math.log(3.0) - 2.3025851 * jax.random.uniform(streams_of[5], (D, FW // TILE), jnp.float32) ** steps_of(streams_of[5], (D, FW // TILE), ((0, 8), (1, 2)), -0.2, 0.2)), 0.3, 3.0),
        "up_q": noise(streams_of[6], (D, FW), D ** -0.5, 0.078125, ((0, 8), (1, 2))),
        "up_scale": jnp.clip(jnp.exp(math.log(3.0) - 2.3025851 * jax.random.uniform(streams_of[7], (D, FW // TILE), jnp.float32) ** steps_of(streams_of[7], (D, FW // TILE), ((0, 8), (1, 2)), -0.2, 0.2)), 0.3, 3.0),
        "down_q": noise(streams_of[8], (FW, D), FW ** -0.5, 0.21875, ((0, 2), (1, 8))),
        "down_scale": jnp.clip(jnp.exp(math.log(3.0) - 2.3025851 * jax.random.uniform(streams_of[9], (FW // TILE, D), jnp.float32) ** steps_of(streams_of[9], (FW // TILE, D), ((0, 2), (1, 8)), -0.2, 0.2)), 0.3, 3.0),
    }


def dequantize(values, scales, tile_axis):
    tile_len = values.shape[tile_axis] // scales.shape[tile_axis]
    return (values.astype(jnp.float32) * jnp.repeat(scales, tile_len, axis=tile_axis)).astype(jnp.bfloat16)


def reference(tokens, expert_ids, combine, row_list, gate_q, gate_scale, up_q, up_scale, down_q, down_scale):
    owner_index = jnp.arange(TOKENS, dtype=jnp.int32) // TOK_DEV
    listed = row_list >= 0
    source_row = jnp.where(listed, row_list + owner_index * TOK_DEV, 0).astype(jnp.int32)
    routed_rows = tokens[source_row]
    slot_hits = jnp.where(expert_ids[source_row] == 0, combine[source_row], jnp.zeros_like(combine[source_row]))
    row_weight = jnp.where(listed, jnp.sum(slot_hits, axis=1), jnp.zeros_like(slot_hits[:, 0]))
    gate_act = jnp.dot(routed_rows, dequantize(gate_q, gate_scale, 1), preferred_element_type=jnp.float32)
    up_act = jnp.dot(routed_rows, dequantize(up_q, up_scale, 1), preferred_element_type=jnp.float32)
    hidden = (jax.nn.silu(gate_act) * up_act).astype(jnp.bfloat16)
    down_w = dequantize(down_q, down_scale, 0)
    hidden_share = FW // N_TENSOR
    summed = jnp.zeros((TOKENS, D), jnp.float32)
    for shard_index in range(N_TENSOR):
        lower = shard_index * hidden_share
        partial_value = jnp.dot(hidden[:, lower:lower + hidden_share], down_w[lower:lower + hidden_share], preferred_element_type=jnp.float32)
        partial_value = partial_value * row_weight[:, None]
        rounded = lax.optimization_barrier(partial_value.astype(jnp.bfloat16))
        summed = summed + rounded.astype(jnp.float32)
    mixed = summed.astype(jnp.bfloat16)
    target_row = jnp.where(listed, source_row, TOKENS).astype(jnp.int32)
    return jnp.zeros((TOKENS, D), jnp.bfloat16).at[target_row].set(mixed, mode="drop")
```

```python
import functools

import jax
import jax.numpy as jnp
from jax import lax
from jax.experimental import pallas as pl
from jax.experimental.pallas import tpu as pltpu
from jax.sharding import PartitionSpec as P

MESH = pl.DeviceIdType.MESH
F32 = jnp.float32
BF16 = jnp.bfloat16


def dequantize(values, scales, tile_axis):
    tile_len = values.shape[tile_axis] // scales.shape[tile_axis]
    return (values.astype(F32) * jnp.repeat(scales, tile_len, axis=tile_axis)).astype(BF16)


def general_body(
    tokens, expert_ids, combine, row_list, gate_q, gate_scale, up_q, up_scale, down_q, down_scale
):
    del row_list
    full_tokens = lax.all_gather(tokens, "tensor", axis=1, tiled=True)
    row_weight = jnp.sum(jnp.where(expert_ids == 0, combine, 0.0), axis=1)
    gate_w = lax.all_gather(dequantize(gate_q, gate_scale, 1), "dp", axis=0, tiled=True)
    up_w = lax.all_gather(dequantize(up_q, up_scale, 1), "dp", axis=0, tiled=True)
    down_w = lax.all_gather(dequantize(down_q, down_scale, 0), "dp", axis=1, tiled=True)
    gate_act = jnp.dot(full_tokens, gate_w, preferred_element_type=F32)
    up_act = jnp.dot(full_tokens, up_w, preferred_element_type=F32)
    hidden = (jax.nn.silu(gate_act) * up_act).astype(BF16)
    part = jnp.dot(hidden, down_w, preferred_element_type=F32) * row_weight[:, None]
    return lax.psum_scatter(part.astype(BF16), "tensor", scatter_dimension=1, tiled=True)


def kernel(
    nx, nz,
    tok, ids, comb, gq, gs, uq, us, dq, ds,
    out,
    T, W, D, acc, ps, pr, hid, o_own, o_send, o_recv,
    st_send, st_recv, sl, w_send, wx_send, w_recv, d_send, dx_send, dy_send, d_recv,
    p_send, p_recv, q_send, q_recv,
):
    y = lax.axis_index("groups")
    dp = lax.axis_index("dp")
    t = lax.axis_index("tensor")
    z, x = dp // nx, dp % nx
    oy, ot, ox = 1 - y, 1 - t, 1 - x
    rows = out.shape[0]
    half = W.shape[2]
    hd = D.shape[2]
    blk = D.shape[3]
    per_core = nx * nz // 2
    up_ok, down_ok = z < nz - 1, z > 0
    ydev, tdev, xdev = (oy, dp, t), (y, dp, ot), (y, z * nx + ox, t)
    zdev = ((y, dp + nx, t), (y, dp - nx, t))
    zok = (up_ok, down_ok)

    barrier = pltpu.get_barrier_semaphore()
    for dev in (ydev, tdev, xdev):
        pl.semaphore_signal(barrier, inc=1, device_id=dev, device_id_type=MESH)
    for k in range(2):
        @pl.when(zok[k])
        def _():
            pl.semaphore_signal(barrier, inc=1, device_id=zdev[k], device_id_type=MESH)

    def remote(src, dst, s, r, dev):
        return pltpu.make_async_remote_copy(
            src_ref=src, dst_ref=dst, send_sem=s, recv_sem=r, device_id=dev, device_id_type=MESH
        )

    own_tok = pltpu.make_async_copy(tok.at[y], T.at[0, 0], sl)
    tok_y = remote(tok.at[oy], T.at[0, 1], st_send.at[0], st_recv.at[0], ydev)
    tok_t = remote(tok.at[y], T.at[1, 0], st_send.at[1], st_recv.at[1], tdev)
    tok_f = remote(T.at[0, 1], T.at[1, 1], st_send.at[2], st_recv.at[2], tdev)
    own_tok.start()

    def wz(m, k, s):
        b = (z - s if k == 0 else z + s) * nx + x
        return remote(W.at[m, b], W.at[m, b], w_send.at[m, k, s], w_recv.at[m, b], zdev[k])

    def wx(m, zz):
        b = zz * nx + x
        return remote(W.at[m, b], W.at[m, b], wx_send.at[m, zz], w_recv.at[m, b], xdev)

    def w_wait(m, b):
        remote(W.at[m, b], W.at[m, b], wx_send.at[m, 0], w_recv.at[m, b], xdev).wait_recv()

    def dz(h, k, s):
        b = (z - s if k == 0 else z + s) * nx + x
        return remote(D.at[b, h], D.at[b, h], d_send.at[h, k, s], d_recv.at[b, h], zdev[k])

    def dx(zz):
        b = zz * nx + x
        return remote(D.at[b, y], D.at[b, y], dx_send.at[zz], d_recv.at[b, y], xdev)

    def dy(zz):
        b = zz * nx + ox
        return remote(D.at[b, y], D.at[b, y], dy_send.at[zz], d_recv.at[b, y], ydev)

    def d_wait(b, h):
        remote(D.at[b, h], D.at[b, h], dx_send.at[0], d_recv.at[b, h], xdev).wait_recv()

    def scale_block(m, q, s):
        for j in range(s.shape[1]):
            cols = pl.ds(j * 128, 128)
            v = q[pl.ds(y * half, half), cols].astype(F32)
            W[m, dp, :, cols] = (v * s[pl.ds(y * half, half), j : j + 1]).astype(BF16)

    scale_block(0, gq, gs)
    pl.semaphore_wait(barrier, 3 + jnp.where(up_ok, 1, 0) + jnp.where(down_ok, 1, 0))

    def start_own_w(m):
        for k in range(2):
            @pl.when(zok[k])
            def _():
                wz(m, k, 0).start()
        wx(m, z).start()

    start_own_w(0)
    tok_y.start()
    tok_t.start()
    scale_block(1, uq, us)
    start_own_w(1)
    for j in range(ds.shape[0]):
        lo = j * 128
        v = (dq[lo : lo + 128, :].astype(F32) * ds[j : j + 1, :]).astype(BF16)
        while lo < (j + 1) * 128:
            n = min((j + 1) * 128, (lo // hd + 1) * hd) - lo
            D[dp, lo // hd, lo % hd : lo % hd + n, :] = v[lo - j * 128 : lo - j * 128 + n]
            lo += n

    def each_arrival(s, body):
        if s >= nz:
            return

        @pl.when(z - s >= 0)
        def _():
            body(z - s, 0)

        @pl.when(z + s < nz)
        def _():
            body(z + s, 1)

    def w_event(m, s):
        def body(zz, k):
            w_wait(m, zz * nx + x)

            @pl.when(zok[k])
            def _():
                wz(m, k, s).start()

            wx(m, zz).start()

        each_arrival(s, body)

    def start_own_d():
        for i in range(2):
            h = y if i == 0 else oy
            for k in range(2):
                @pl.when(zok[k])
                def _():
                    dz(h, k, 0).start()
            if i == 0:
                dx(z).start()

    def d_event(s):
        def body(zz, k):
            b = zz * nx + x
            for i in range(2):
                h = y if i == 0 else oy
                d_wait(b, h)

                @pl.when(zok[k])
                def _():
                    dz(h, k, s).start()

                if i == 0:
                    dx(zz).start()

        each_arrival(s, body)

    def dy_event(s):
        def body(zz, k):
            d_wait(zz * nx + ox, y)
            dy(zz).start()

        if s == 0:
            body(z, 0)
        else:
            each_arrival(s, body)

    tile = 192

    def partial_act(m):
        for zz in range(nz):
            w_wait(m, zz * nx + ox)
        for who in (1, 0):
            @pl.loop(0, rows // tile)
            def _(i):
                r = pl.ds(pl.multiple_of(i * tile, tile), tile)
                total = None
                for side in range(2):
                    blocks = pl.ds((t if side == 0 else ot) * per_core, per_core)
                    w = W[m, blocks].reshape(per_core * half, W.shape[3])
                    p = jnp.dot(T[side, who, r, :], w, preferred_element_type=F32)
                    total = p if total is None else total + p
                if who == 1:
                    ps[m, r, :] = total.astype(BF16)
                else:
                    acc[m, r, :] = total
            if who == 1:
                pcopy(m).start()

    def pcopy(m):
        return remote(ps.at[m], pr.at[m], p_send.at[m], p_recv.at[m], ydev)

    w_event(0, 1)
    w_event(0, 2)
    w_event(0, 3)
    start_own_d()
    w_event(1, 1)
    tok_y.wait_recv()
    tok_f.start()
    own_tok.wait()
    tok_t.wait_recv()
    w_event(1, 2)
    w_event(1, 3)
    tok_f.wait_recv()
    partial_act(0)
    d_event(1)
    partial_act(1)
    dy_event(0)
    d_event(2)
    dy_event(1)
    for m in range(2):
        pcopy(m).wait_recv()
    for i in range(rows // tile):
        r = slice(i * tile, (i + 1) * tile)
        g = acc[0, r, :] + pr[0, r, :].astype(F32)
        u = acc[1, r, :] + pr[1, r, :].astype(F32)
        hid[r, :] = (g / (1.0 + jnp.exp(-g)) * u).astype(BF16)
    weight = jnp.sum(jnp.where(ids[...] == 0, comb[...], 0.0), axis=1, keepdims=True)

    def qcopy(c):
        return remote(o_send.at[c], o_recv.at[c], q_send.at[c], q_recv.at[c], tdev)

    def down_block(b):
        c = b % per_core
        mine = b // per_core == t
        w = D[b].reshape(2 * hd, blk)
        p = jnp.dot(hid[...], w, preferred_element_type=F32) * weight
        p = p.astype(BF16)

        @pl.when(mine)
        def _():
            o_own[c] = p

        @pl.when(jnp.logical_not(mine))
        def _():
            o_send[c] = p
            qcopy(c).start()

    d_event(3)
    dy_event(2)
    dy_event(3)

    @pl.loop(0, nz)
    def _(k):
        down_block(((z + k) % nz) * nx + x)

    @pl.loop(0, nz)
    def _(k):
        zz = (z + k) % nz
        d_wait(zz * nx + ox, oy)
        down_block(zz * nx + ox)

    for c in range(per_core):
        qcopy(c).wait_recv()
        cols = pl.ds(c * blk, blk)
        out[:, cols] = (o_own[c].astype(F32) + o_recv[c].astype(F32)).astype(BF16)

    tok_y.wait_send()
    tok_t.wait_send()
    tok_f.wait_send()
    for k in range(2):
        for s in range(nz - 1):
            here = (z - s >= 0) if k == 0 else (z + s < nz)

            @pl.when(jnp.logical_and(here, zok[k]))
            def _():
                for m in range(2):
                    wz(m, k, s).wait_send()
                for h in range(2):
                    dz(h, k, s).wait_send()
    for zz in range(nz):
        for m in range(2):
            wx(m, zz).wait_send()
        dx(zz).wait_send()
        dy(zz).wait_send()
    for m in range(2):
        pcopy(m).wait_send()
    for c in range(per_core):
        qcopy(c).wait_send()


def pair_body(
    tokens, expert_ids, combine, row_list, gate_q, gate_scale, up_q, up_scale, down_q, down_scale,
    *, nx, nz
):
    del row_list
    rows, feats = tokens.shape
    depth, width = gate_q.shape
    half = depth // 2
    blocks = nx * nz
    per_core = blocks // 2
    hd = down_q.shape[0] // 2
    blk = down_q.shape[1]
    tok = tokens.reshape(rows, per_core, 2, half).transpose(2, 0, 1, 3).reshape(2, rows, feats // 2)
    vmem = pl.BlockSpec(memory_space=pltpu.VMEM)
    dma = pltpu.SemaphoreType.DMA
    return pl.pallas_call(
        functools.partial(kernel, nx, nz),
        out_shape=jax.ShapeDtypeStruct((rows, feats), BF16),
        in_specs=[pl.BlockSpec(memory_space=pl.ANY)] + [vmem] * 8,
        out_specs=vmem,
        scratch_shapes=[
            pltpu.VMEM((2, 2, rows, feats // 2), BF16),
            pltpu.VMEM((2, blocks, half, width), BF16),
            pltpu.VMEM((blocks, 2, hd, blk), BF16),
            pltpu.VMEM((2, rows, width), F32),
            pltpu.VMEM((2, rows, width), BF16),
            pltpu.VMEM((2, rows, width), BF16),
            pltpu.VMEM((rows, width), BF16),
            pltpu.VMEM((per_core, rows, blk), BF16),
            pltpu.VMEM((per_core, rows, blk), BF16),
            pltpu.VMEM((per_core, rows, blk), BF16),
            dma((3,)), dma((3,)), dma,
            dma((2, 2, nz)), dma((2, nz)), dma((2, blocks)),
            dma((2, 2, nz)), dma((nz,)), dma((nz,)), dma((blocks, 2)),
            dma((2,)), dma((2,)), dma((per_core,)), dma((per_core,)),
        ],
        compiler_params=pltpu.CompilerParams(
            collective_id=0, has_side_effects=True, vmem_limit_bytes=56 * 1024 * 1024
        ),
        cost_estimate=pl.CostEstimate(
            flops=6 * rows * width * depth * blocks, bytes_accessed=40_000_000, transcendentals=rows * width
        ),
    )(tok, expert_ids, combine, gate_q, gate_scale, up_q, up_scale, down_q, down_scale)


def solution(mesh):
    placed = (
        P(("groups", "dp"), "tensor"),
        P(("groups", "dp"), None),
        P(("groups", "dp"), None),
        P(("groups", "dp")),
        P("dp", "tensor"),
        P("dp", "tensor"),
        P("dp", "tensor"),
        P("dp", "tensor"),
        P("tensor", "dp"),
        P("tensor", "dp"),
    )
    sizes = tuple(mesh.shape[a] for a in ("groups", "dp", "tensor"))
    body = functools.partial(pair_body, nx=2, nz=4) if sizes == (2, 8, 2) else general_body
    return jax.shard_map(
        body, mesh=mesh, in_specs=placed, out_specs=P(("groups", "dp"), "tensor"), check_vma=False
    )
```

```python
import functools

import jax
import jax.numpy as jnp
from jax import lax
from jax.experimental import pallas as pl
from jax.experimental.pallas import tpu as pltpu
from jax.sharding import PartitionSpec as P

MESH = pl.DeviceIdType.MESH
F32 = jnp.float32
BF16 = jnp.bfloat16


def dequantize(values, scales, tile_axis):
    tile_len = values.shape[tile_axis] // scales.shape[tile_axis]
    return (values.astype(F32) * jnp.repeat(scales, tile_len, axis=tile_axis)).astype(BF16)


def general_body(
    tokens, expert_ids, combine, row_list, gate_q, gate_scale, up_q, up_scale, down_q, down_scale
):
    del row_list
    full_tokens = lax.all_gather(tokens, "tensor", axis=1, tiled=True)
    row_weight = jnp.sum(jnp.where(expert_ids == 0, combine, 0.0), axis=1)
    gate_w = lax.all_gather(dequantize(gate_q, gate_scale, 1), "dp", axis=0, tiled=True)
    up_w = lax.all_gather(dequantize(up_q, up_scale, 1), "dp", axis=0, tiled=True)
    down_w = lax.all_gather(dequantize(down_q, down_scale, 0), "dp", axis=1, tiled=True)
    gate_act = jnp.dot(full_tokens, gate_w, preferred_element_type=F32)
    up_act = jnp.dot(full_tokens, up_w, preferred_element_type=F32)
    hidden = (jax.nn.silu(gate_act) * up_act).astype(BF16)
    part = jnp.dot(hidden, down_w, preferred_element_type=F32) * row_weight[:, None]
    return lax.psum_scatter(part.astype(BF16), "tensor", scatter_dimension=1, tiled=True)


def kernel(
    nx, nz,
    tok, ids, comb, gq, gs, uq, us, dq, ds,
    out,
    T, W, D, wt, acc, ps, pr, hid, o_own, o_send, o_recv,
    st_send, st_recv, f_send, f_recv, sl, w_send, wx_send, w_recv, d_send, dx_send, dy_send, d_recv,
    p_send, p_recv, q_send, q_recv,
):
    y = lax.axis_index("groups")
    dp = lax.axis_index("dp")
    t = lax.axis_index("tensor")
    z, x = dp // nx, dp % nx
    oy, ot, ox = 1 - y, 1 - t, 1 - x
    rows = out.shape[0]
    win = W.shape[2]
    depth = gq.shape[0]
    half = depth // 2
    pad = win - half
    real = pl.ds(pl.multiple_of(y * pad, pad), half)
    zero = pl.ds(pl.multiple_of((1 - y) * half, pad), pad)
    hd = D.shape[2]
    blk = D.shape[3]
    per_core = nx * nz // 2
    up_ok, down_ok = z < nz - 1, z > 0
    ydev, tdev, xdev = (oy, dp, t), (y, dp, ot), (y, z * nx + ox, t)
    zdev = ((y, dp + nx, t), (y, dp - nx, t))
    zok = (up_ok, down_ok)

    barrier = pltpu.get_barrier_semaphore()
    for dev in (ydev, tdev, xdev):
        pl.semaphore_signal(barrier, inc=1, device_id=dev, device_id_type=MESH)
    for k in range(2):
        @pl.when(zok[k])
        def _():
            pl.semaphore_signal(barrier, inc=1, device_id=zdev[k], device_id_type=MESH)

    def remote(src, dst, s, r, dev):
        return pltpu.make_async_remote_copy(
            src_ref=src, dst_ref=dst, send_sem=s, recv_sem=r, device_id=dev, device_id_type=MESH
        )

    def feats(j, v):
        return tok.at[:, pl.ds(pl.multiple_of(j * depth + v * (depth - win), 128), win)]

    def slot(side, who, j):
        return T.at[side, who, :, pl.ds(j * win, win)]

    def own_tok(j):
        return pltpu.make_async_copy(feats(j, y), slot(0, 0, j), sl.at[j])

    def tok_y(j):
        return remote(feats(j, oy), slot(0, 1, j), st_send.at[0, j], st_recv.at[0, j], ydev)

    def tok_t(j):
        return remote(feats(j, y), slot(1, 0, j), st_send.at[1, j], st_recv.at[1, j], tdev)

    tok_f = remote(T.at[0, 1], T.at[1, 1], f_send, f_recv, tdev)
    for j in range(per_core):
        own_tok(j).start()

    def wz(m, k, s):
        b = (z - s if k == 0 else z + s) * nx + x
        ref = W.at[m, b, real]
        return remote(ref, ref, w_send.at[m, k, s], w_recv.at[m, b], zdev[k])

    def wx(m, zz):
        b = zz * nx + x
        ref = W.at[m, b, real]
        return remote(ref, ref, wx_send.at[m, zz], w_recv.at[m, b], xdev)

    def w_wait(m, b):
        ref = W.at[m, b, real]
        remote(ref, ref, wx_send.at[m, 0], w_recv.at[m, b], xdev).wait_recv()

    def dz(h, k, s):
        b = (z - s if k == 0 else z + s) * nx + x
        return remote(D.at[b, h], D.at[b, h], d_send.at[h, k, s], d_recv.at[b, h], zdev[k])

    def dx(zz):
        b = zz * nx + x
        return remote(D.at[b, y], D.at[b, y], dx_send.at[zz], d_recv.at[b, y], xdev)

    def dy(zz):
        b = zz * nx + ox
        return remote(D.at[b, y], D.at[b, y], dy_send.at[zz], d_recv.at[b, y], ydev)

    def d_wait(b, h):
        remote(D.at[b, h], D.at[b, h], dx_send.at[0], d_recv.at[b, h], xdev).wait_recv()

    def spread(row):
        return jnp.broadcast_to(row, (128, row.shape[1])).T

    def scale_block(m, q, s):
        first = pl.multiple_of(y * (depth - win), 128)
        for j in range(s.shape[0]):
            cols = pl.ds(j * 128, 128)
            v = q[pl.ds(first, win), cols].astype(F32)
            W[m, dp, :, cols] = (v * spread(s[j : j + 1, pl.ds(first, win)])).astype(BF16)

    scale_block(0, gq, gs)
    pl.semaphore_wait(barrier, 3 + jnp.where(up_ok, 1, 0) + jnp.where(down_ok, 1, 0))

    def start_own_w(m):
        for k in range(2):
            @pl.when(zok[k])
            def _():
                wz(m, k, 0).start()
        wx(m, z).start()

    start_own_w(0)
    for j in range(per_core):
        tok_y(j).start()
        tok_t(j).start()
    scale_block(1, uq, us)
    start_own_w(1)
    for j in range(ds.shape[0]):
        lo = j * 128
        v = (dq[lo : lo + 128, :].astype(F32) * ds[j : j + 1, :]).astype(BF16)
        while lo < (j + 1) * 128:
            n = min((j + 1) * 128, (lo // hd + 1) * hd) - lo
            D[dp, lo // hd, lo % hd : lo % hd + n, :] = v[lo - j * 128 : lo - j * 128 + n]
            lo += n

    def each_arrival(s, body):
        if s >= nz:
            return

        @pl.when(z - s >= 0)
        def _():
            body(z - s, 0)

        @pl.when(z + s < nz)
        def _():
            body(z + s, 1)

    def w_event(m, s):
        def body(zz, k):
            w_wait(m, zz * nx + x)

            @pl.when(zok[k])
            def _():
                wz(m, k, s).start()

            wx(m, zz).start()

        each_arrival(s, body)

    def start_own_d():
        for i in range(2):
            h = y if i == 0 else oy
            for k in range(2):
                @pl.when(zok[k])
                def _():
                    dz(h, k, 0).start()
            if i == 0:
                dx(z).start()

    def d_event(s):
        def body(zz, k):
            b = zz * nx + x
            for i in range(2):
                h = y if i == 0 else oy
                d_wait(b, h)

                @pl.when(zok[k])
                def _():
                    dz(h, k, s).start()

                if i == 0:
                    dx(zz).start()

        each_arrival(s, body)

    def dy_event(s):
        def body(zz, k):
            d_wait(zz * nx + ox, y)
            dy(zz).start()

        if s == 0:
            body(z, 0)
        else:
            each_arrival(s, body)

    tile = 192

    def partial_act(m):
        for zz in range(nz):
            w_wait(m, zz * nx + ox)
        for who in (1, 0):
            @pl.loop(0, rows // tile)
            def _(i):
                r = pl.ds(pl.multiple_of(i * tile, tile), tile)
                total = None
                for side in range(2):
                    blocks = pl.ds((t if side == 0 else ot) * per_core, per_core)
                    w = W[m, blocks].reshape(per_core * win, W.shape[3])
                    p = jnp.dot(T[side, who, r, :], w, preferred_element_type=F32)
                    total = p if total is None else total + p
                if who == 1:
                    ps[m, r, :] = total.astype(BF16)
                else:
                    acc[m, r, :] = total
            if who == 1:
                pcopy(m).start()

    def pcopy(m):
        return remote(ps.at[m], pr.at[m], p_send.at[m], p_recv.at[m], ydev)

    for m in range(2):
        @pl.loop(0, nx * nz)
        def _(b):
            W[m, b, zero] = jnp.zeros((pad, W.shape[3]), BF16)
    wt[...] = spread(jnp.sum(jnp.where(ids[...] == 0, comb[...], 0.0), axis=0, keepdims=True))

    w_event(0, 1)
    w_event(0, 2)
    w_event(0, 3)
    start_own_d()
    w_event(1, 1)
    for j in range(per_core):
        tok_y(j).wait_recv()
    tok_f.start()
    for j in range(per_core):
        own_tok(j).wait()
        tok_t(j).wait_recv()
    w_event(1, 2)
    w_event(1, 3)
    tok_f.wait_recv()
    partial_act(0)
    d_event(1)
    partial_act(1)
    dy_event(0)
    d_event(2)
    dy_event(1)
    for m in range(2):
        pcopy(m).wait_recv()
    for i in range(rows // tile):
        r = slice(i * tile, (i + 1) * tile)
        g = acc[0, r, :] + pr[0, r, :].astype(F32)
        u = acc[1, r, :] + pr[1, r, :].astype(F32)
        hid[r, :] = (g / (1.0 + jnp.exp(-g)) * u).astype(BF16)

    def qcopy(c):
        return remote(o_send.at[c], o_recv.at[c], q_send.at[c], q_recv.at[c], tdev)

    def down_block(b):
        c = b % per_core
        mine = b // per_core == t
        w = D[b].reshape(2 * hd, blk)
        p = jnp.dot(hid[...], w, preferred_element_type=F32)
        p = [(p[:, i : i + 128] * wt[...]).astype(BF16) for i in range(0, blk, 128)]

        @pl.when(mine)
        def _():
            for i, v in enumerate(p):
                o_own[c, :, i * 128 : (i + 1) * 128] = v

        @pl.when(jnp.logical_not(mine))
        def _():
            for i, v in enumerate(p):
                o_send[c, :, i * 128 : (i + 1) * 128] = v
            qcopy(c).start()

    d_event(3)
    dy_event(2)
    dy_event(3)

    @pl.loop(0, nz)
    def _(k):
        down_block(((z + k) % nz) * nx + x)

    @pl.loop(0, nz)
    def _(k):
        zz = (z + k) % nz
        d_wait(zz * nx + ox, oy)
        down_block(zz * nx + ox)

    for c in range(per_core):
        qcopy(c).wait_recv()
        cols = pl.ds(c * blk, blk)
        out[:, cols] = (o_own[c].astype(F32) + o_recv[c].astype(F32)).astype(BF16)

    for j in range(per_core):
        tok_y(j).wait_send()
        tok_t(j).wait_send()
    tok_f.wait_send()
    for k in range(2):
        for s in range(nz - 1):
            here = (z - s >= 0) if k == 0 else (z + s < nz)

            @pl.when(jnp.logical_and(here, zok[k]))
            def _():
                for m in range(2):
                    wz(m, k, s).wait_send()
                for h in range(2):
                    dz(h, k, s).wait_send()
    for zz in range(nz):
        for m in range(2):
            wx(m, zz).wait_send()
        dx(zz).wait_send()
        dy(zz).wait_send()
    for m in range(2):
        pcopy(m).wait_send()
    for c in range(per_core):
        qcopy(c).wait_send()


def pair_body(
    tokens, expert_ids, combine, row_list, gate_q, gate_scale, up_q, up_scale, down_q, down_scale,
    *, nx, nz
):
    del row_list
    rows, feats = tokens.shape
    depth, width = gate_q.shape
    win = -(-(depth // 2) // 128) * 128
    blocks = nx * nz
    per_core = blocks // 2
    hd = down_q.shape[0] // 2
    blk = down_q.shape[1]
    vmem = pl.BlockSpec(memory_space=pltpu.VMEM)
    dma = pltpu.SemaphoreType.DMA
    return pl.pallas_call(
        functools.partial(kernel, nx, nz),
        out_shape=jax.ShapeDtypeStruct((rows, feats), BF16),
        in_specs=[pl.BlockSpec(memory_space=pl.ANY)] + [vmem] * 8,
        out_specs=vmem,
        scratch_shapes=[
            pltpu.VMEM((2, 2, rows, per_core * win), BF16),
            pltpu.VMEM((2, blocks, win, width), BF16),
            pltpu.VMEM((blocks, 2, hd, blk), BF16),
            pltpu.VMEM((rows, 128), F32),
            pltpu.VMEM((2, rows, width), F32),
            pltpu.VMEM((2, rows, width), BF16),
            pltpu.VMEM((2, rows, width), BF16),
            pltpu.VMEM((rows, width), BF16),
            pltpu.VMEM((per_core, rows, blk), BF16),
            pltpu.VMEM((per_core, rows, blk), BF16),
            pltpu.VMEM((per_core, rows, blk), BF16),
            dma((2, per_core)), dma((2, per_core)), dma, dma, dma((per_core,)),
            dma((2, 2, nz)), dma((2, nz)), dma((2, blocks)),
            dma((2, 2, nz)), dma((nz,)), dma((nz,)), dma((blocks, 2)),
            dma((2,)), dma((2,)), dma((per_core,)), dma((per_core,)),
        ],
        compiler_params=pltpu.CompilerParams(
            collective_id=0, has_side_effects=True, vmem_limit_bytes=40 * 1024 * 1024
        ),
        cost_estimate=pl.CostEstimate(
            flops=6 * rows * width * depth * blocks, bytes_accessed=40_000_000, transcendentals=rows * width
        ),
    )(tokens, expert_ids.T, combine.T, gate_q, gate_scale.T, up_q, up_scale.T, down_q, down_scale)


def solution(mesh):
    placed = (
        P(("groups", "dp"), "tensor"),
        P(("groups", "dp"), None),
        P(("groups", "dp"), None),
        P(("groups", "dp")),
        P("dp", "tensor"),
        P("dp", "tensor"),
        P("dp", "tensor"),
        P("dp", "tensor"),
        P("tensor", "dp"),
        P("tensor", "dp"),
    )
    sizes = tuple(mesh.shape[a] for a in ("groups", "dp", "tensor"))
    body = functools.partial(pair_body, nx=2, nz=4) if sizes == (2, 8, 2) else general_body
    return jax.shard_map(
        body, mesh=mesh, in_specs=placed, out_specs=P(("groups", "dp"), "tensor"), check_vma=False
    )
```

```python
import functools

import jax
import jax.numpy as jnp
from jax import lax
from jax.experimental import pallas as pl
from jax.experimental.pallas import tpu as pltpu
from jax.sharding import PartitionSpec as P

MESH = pl.DeviceIdType.MESH
F32 = jnp.float32
BF16 = jnp.bfloat16


def dequantize(values, scales, tile_axis):
    tile_len = values.shape[tile_axis] // scales.shape[tile_axis]
    return (values.astype(F32) * jnp.repeat(scales, tile_len, axis=tile_axis)).astype(BF16)


def general_body(
    tokens, expert_ids, combine, row_list, gate_q, gate_scale, up_q, up_scale, down_q, down_scale
):
    del row_list
    full_tokens = lax.all_gather(tokens, "tensor", axis=1, tiled=True)
    row_weight = jnp.sum(jnp.where(expert_ids == 0, combine, 0.0), axis=1)
    gate_w = lax.all_gather(dequantize(gate_q, gate_scale, 1), "dp", axis=0, tiled=True)
    up_w = lax.all_gather(dequantize(up_q, up_scale, 1), "dp", axis=0, tiled=True)
    down_w = lax.all_gather(dequantize(down_q, down_scale, 0), "dp", axis=1, tiled=True)
    gate_act = jnp.dot(full_tokens, gate_w, preferred_element_type=F32)
    up_act = jnp.dot(full_tokens, up_w, preferred_element_type=F32)
    hidden = (jax.nn.silu(gate_act) * up_act).astype(BF16)
    part = jnp.dot(hidden, down_w, preferred_element_type=F32) * row_weight[:, None]
    return lax.psum_scatter(part.astype(BF16), "tensor", scatter_dimension=1, tiled=True)


def kernel(
    nx, nz,
    tok, ids_h, comb_h, gq_h, gs_h, uq_h, us_h, dq_h, ds_h,
    out,
    gs, gq, us, uq, ds, dq, ids, comb, in_sem, T, W, D, wt, acc, ps, pr, hid, o_own, o_send, o_recv,
    st_send, st_recv, f_send, f_recv, sl, w_send, wx_send, w_recv, d_send, dx_send, dy_send, d_recv,
    p_send, p_recv, q_send, q_recv,
):
    y = lax.axis_index("groups")
    dp = lax.axis_index("dp")
    t = lax.axis_index("tensor")
    z, x = dp // nx, dp % nx
    oy, ot, ox = 1 - y, 1 - t, 1 - x
    rows = out.shape[0]
    win = W.shape[2]
    depth = gq.shape[0]
    half = depth // 2
    pad = win - half
    real = pl.ds(pl.multiple_of(y * pad, pad), half)
    zero = pl.ds(pl.multiple_of((1 - y) * half, pad), pad)
    hd = D.shape[2]
    blk = D.shape[3]
    per_core = nx * nz // 2
    up_ok, down_ok = z < nz - 1, z > 0
    ydev, tdev, xdev = (oy, dp, t), (y, dp, ot), (y, z * nx + ox, t)
    zdev = ((y, dp + nx, t), (y, dp - nx, t))
    zok = (up_ok, down_ok)

    sources = (gs_h, gq_h, us_h, uq_h, ds_h, dq_h, ids_h, comb_h)
    targets = (gs, gq, us, uq, ds, dq, ids, comb)
    loads = [pltpu.make_async_copy(a, b, in_sem.at[i]) for i, (a, b) in enumerate(zip(sources, targets))]
    for load in loads:
        load.start()

    barrier = pltpu.get_barrier_semaphore()
    for dev in (ydev, tdev, xdev):
        pl.semaphore_signal(barrier, inc=1, device_id=dev, device_id_type=MESH)
    for k in range(2):
        @pl.when(zok[k])
        def _():
            pl.semaphore_signal(barrier, inc=1, device_id=zdev[k], device_id_type=MESH)

    def remote(src, dst, s, r, dev):
        return pltpu.make_async_remote_copy(
            src_ref=src, dst_ref=dst, send_sem=s, recv_sem=r, device_id=dev, device_id_type=MESH
        )

    def feats(j, v):
        return tok.at[:, pl.ds(pl.multiple_of(j * depth + v * (depth - win), 128), win)]

    def slot(side, who, j):
        return T.at[side, who, :, pl.ds(j * win, win)]

    def own_tok(j):
        return pltpu.make_async_copy(feats(j, y), slot(0, 0, j), sl.at[j])

    def tok_y(j):
        return remote(feats(j, oy), slot(0, 1, j), st_send.at[0, j], st_recv.at[0, j], ydev)

    def tok_t(j):
        return remote(feats(j, y), slot(1, 0, j), st_send.at[1, j], st_recv.at[1, j], tdev)

    tok_f = remote(T.at[0, 1], T.at[1, 1], f_send, f_recv, tdev)
    for j in range(per_core):
        own_tok(j).start()

    def wz(m, k, s):
        b = (z - s if k == 0 else z + s) * nx + x
        ref = W.at[m, b, real]
        return remote(ref, ref, w_send.at[m, k, s], w_recv.at[m, b], zdev[k])

    def wx(m, zz):
        b = zz * nx + x
        ref = W.at[m, b, real]
        return remote(ref, ref, wx_send.at[m, zz], w_recv.at[m, b], xdev)

    def w_wait(m, b):
        ref = W.at[m, b, real]
        remote(ref, ref, wx_send.at[m, 0], w_recv.at[m, b], xdev).wait_recv()

    def dz(h, k, s):
        b = (z - s if k == 0 else z + s) * nx + x
        return remote(D.at[b, h], D.at[b, h], d_send.at[h, k, s], d_recv.at[b, h], zdev[k])

    def dx(zz):
        b = zz * nx + x
        return remote(D.at[b, y], D.at[b, y], dx_send.at[zz], d_recv.at[b, y], xdev)

    def dy(zz):
        b = zz * nx + ox
        return remote(D.at[b, y], D.at[b, y], dy_send.at[zz], d_recv.at[b, y], ydev)

    def d_wait(b, h):
        remote(D.at[b, h], D.at[b, h], dx_send.at[0], d_recv.at[b, h], xdev).wait_recv()

    def spread(row):
        return jnp.broadcast_to(row, (128, row.shape[1])).T

    def scale_block(m, q, s):
        first = pl.multiple_of(y * (depth - win), 128)
        for j in range(s.shape[0]):
            cols = pl.ds(j * 128, 128)
            v = q[pl.ds(first, win), cols].astype(F32)
            W[m, dp, :, cols] = (v * spread(s[j : j + 1, pl.ds(first, win)])).astype(BF16)

    loads[0].wait()
    loads[1].wait()
    scale_block(0, gq, gs)
    pl.semaphore_wait(barrier, 3 + jnp.where(up_ok, 1, 0) + jnp.where(down_ok, 1, 0))

    def start_own_w(m):
        for k in range(2):
            @pl.when(zok[k])
            def _():
                wz(m, k, 0).start()
        wx(m, z).start()

    start_own_w(0)
    for j in range(per_core):
        tok_y(j).start()
        tok_t(j).start()
    loads[2].wait()
    loads[3].wait()
    scale_block(1, uq, us)
    start_own_w(1)
    loads[4].wait()
    loads[5].wait()
    for j in range(ds.shape[0]):
        lo = j * 128
        v = (dq[lo : lo + 128, :].astype(F32) * ds[j : j + 1, :]).astype(BF16)
        while lo < (j + 1) * 128:
            n = min((j + 1) * 128, (lo // hd + 1) * hd) - lo
            D[dp, lo // hd, lo % hd : lo % hd + n, :] = v[lo - j * 128 : lo - j * 128 + n]
            lo += n

    def each_arrival(s, body):
        if s >= nz:
            return

        @pl.when(z - s >= 0)
        def _():
            body(z - s, 0)

        @pl.when(z + s < nz)
        def _():
            body(z + s, 1)

    def w_event(m, s):
        def body(zz, k):
            w_wait(m, zz * nx + x)

            @pl.when(zok[k])
            def _():
                wz(m, k, s).start()

            wx(m, zz).start()

        each_arrival(s, body)

    def start_own_d(h):
        for k in range(2):
            @pl.when(zok[k])
            def _():
                dz(h, k, 0).start()

    def d_event(h, s, cross):
        def body(zz, k):
            d_wait(zz * nx + x, h)

            @pl.when(zok[k])
            def _():
                dz(h, k, s).start()

            if cross:
                dx(zz).start()

        each_arrival(s, body)

    def dy_event(s):
        def body(zz, k):
            d_wait(zz * nx + ox, y)
            dy(zz).start()

        if s == 0:
            body(z, 0)
        else:
            each_arrival(s, body)

    tile = 192

    def partial_act(m):
        for zz in range(nz):
            w_wait(m, zz * nx + ox)
        for who in (1, 0):
            @pl.loop(0, rows // tile)
            def _(i):
                r = pl.ds(pl.multiple_of(i * tile, tile), tile)
                total = None
                for side in range(2):
                    blocks = pl.ds((t if side == 0 else ot) * per_core, per_core)
                    w = W[m, blocks].reshape(per_core * win, W.shape[3])
                    p = jnp.dot(T[side, who, r, :], w, preferred_element_type=F32)
                    total = p if total is None else total + p
                if who == 1:
                    ps[m, r, :] = total.astype(BF16)
                else:
                    acc[m, r, :] = total
            if who == 1:
                pcopy(m).start()

    def pcopy(m):
        return remote(ps.at[m], pr.at[m], p_send.at[m], p_recv.at[m], ydev)

    for m in range(2):
        @pl.loop(0, nx * nz)
        def _(b):
            W[m, b, zero] = jnp.zeros((pad, W.shape[3]), BF16)
    loads[6].wait()
    loads[7].wait()
    wt[...] = spread(jnp.sum(jnp.where(ids[...] == 0, comb[...], 0.0), axis=0, keepdims=True))

    w_event(0, 1)
    w_event(0, 2)
    start_own_d(y)
    w_event(0, 3)
    dx(z).start()
    w_event(1, 1)
    for j in range(per_core):
        tok_y(j).wait_recv()
    tok_f.start()
    for j in range(per_core):
        own_tok(j).wait()
        tok_t(j).wait_recv()
    d_event(y, 1, True)
    w_event(1, 2)
    tok_f.wait_recv()
    partial_act(0)
    dy_event(0)
    w_event(1, 3)
    d_event(y, 2, True)
    start_own_d(oy)
    dy_event(1)
    d_event(y, 3, True)
    d_event(oy, 1, False)
    partial_act(1)
    dy_event(2)
    d_event(oy, 2, False)
    for m in range(2):
        pcopy(m).wait_recv()
    for i in range(rows // tile):
        r = slice(i * tile, (i + 1) * tile)
        g = acc[0, r, :] + pr[0, r, :].astype(F32)
        u = acc[1, r, :] + pr[1, r, :].astype(F32)
        hid[r, :] = (g / (1.0 + jnp.exp(-g)) * u).astype(BF16)

    def qcopy(c):
        return remote(o_send.at[c], o_recv.at[c], q_send.at[c], q_recv.at[c], tdev)

    def down_block(b):
        c = b % per_core
        mine = b // per_core == t
        w = D[b].reshape(2 * hd, blk)
        p = jnp.dot(hid[...], w, preferred_element_type=F32)
        p = [(p[:, i : i + 128] * wt[...]).astype(BF16) for i in range(0, blk, 128)]

        @pl.when(mine)
        def _():
            for i, v in enumerate(p):
                o_own[c, :, i * 128 : (i + 1) * 128] = v

        @pl.when(jnp.logical_not(mine))
        def _():
            for i, v in enumerate(p):
                o_send[c, :, i * 128 : (i + 1) * 128] = v
            qcopy(c).start()

    def nearest(k):
        low = jnp.where(k <= z, z - k, k)
        high = jnp.where(k <= nz - 1 - z, z + k, nz - 1 - k)
        return jnp.where(2 * z < nz, low, high)

    dy_event(3)
    d_event(oy, 3, False)

    @pl.loop(0, nz)
    def _(k):
        down_block(nearest(k) * nx + x)

    @pl.loop(0, nz)
    def _(k):
        zz = nearest(k)
        d_wait(zz * nx + ox, oy)
        down_block(zz * nx + ox)

    for c in range(per_core):
        qcopy(c).wait_recv()
        cols = pl.ds(c * blk, blk)
        out[:, cols] = (o_own[c].astype(F32) + o_recv[c].astype(F32)).astype(BF16)

    for j in range(per_core):
        tok_y(j).wait_send()
        tok_t(j).wait_send()
    tok_f.wait_send()
    for k in range(2):
        for s in range(nz - 1):
            here = (z - s >= 0) if k == 0 else (z + s < nz)

            @pl.when(jnp.logical_and(here, zok[k]))
            def _():
                for m in range(2):
                    wz(m, k, s).wait_send()
                for h in range(2):
                    dz(h, k, s).wait_send()
    for zz in range(nz):
        for m in range(2):
            wx(m, zz).wait_send()
        dx(zz).wait_send()
        dy(zz).wait_send()
    for m in range(2):
        pcopy(m).wait_send()
    for c in range(per_core):
        qcopy(c).wait_send()


def pair_body(
    tokens, expert_ids, combine, row_list, gate_q, gate_scale, up_q, up_scale, down_q, down_scale,
    *, nx, nz
):
    del row_list
    rows, feats = tokens.shape
    depth, width = gate_q.shape
    win = -(-(depth // 2) // 128) * 128
    blocks = nx * nz
    per_core = blocks // 2
    hd = down_q.shape[0] // 2
    blk = down_q.shape[1]
    vmem = pl.BlockSpec(memory_space=pltpu.VMEM)
    dma = pltpu.SemaphoreType.DMA
    return pl.pallas_call(
        functools.partial(kernel, nx, nz),
        out_shape=jax.ShapeDtypeStruct((rows, feats), BF16),
        in_specs=[pl.BlockSpec(memory_space=pltpu.HBM)] * 9,
        out_specs=vmem,
        scratch_shapes=[
            pltpu.VMEM(gate_scale.shape[::-1], F32),
            pltpu.VMEM(gate_q.shape, BF16),
            pltpu.VMEM(up_scale.shape[::-1], F32),
            pltpu.VMEM(up_q.shape, BF16),
            pltpu.VMEM(down_scale.shape, F32),
            pltpu.VMEM(down_q.shape, BF16),
            pltpu.VMEM(expert_ids.shape[::-1], jnp.int32),
            pltpu.VMEM(combine.shape[::-1], F32),
            dma((8,)),
            pltpu.VMEM((2, 2, rows, per_core * win), BF16),
            pltpu.VMEM((2, blocks, win, width), BF16),
            pltpu.VMEM((blocks, 2, hd, blk), BF16),
            pltpu.VMEM((rows, 128), F32),
            pltpu.VMEM((2, rows, width), F32),
            pltpu.VMEM((2, rows, width), BF16),
            pltpu.VMEM((2, rows, width), BF16),
            pltpu.VMEM((rows, width), BF16),
            pltpu.VMEM((per_core, rows, blk), BF16),
            pltpu.VMEM((per_core, rows, blk), BF16),
            pltpu.VMEM((per_core, rows, blk), BF16),
            dma((2, per_core)), dma((2, per_core)), dma, dma, dma((per_core,)),
            dma((2, 2, nz)), dma((2, nz)), dma((2, blocks)),
            dma((2, 2, nz)), dma((nz,)), dma((nz,)), dma((blocks, 2)),
            dma((2,)), dma((2,)), dma((per_core,)), dma((per_core,)),
        ],
        compiler_params=pltpu.CompilerParams(
            collective_id=0, has_side_effects=True, vmem_limit_bytes=56 * 1024 * 1024
        ),
        cost_estimate=pl.CostEstimate(
            flops=6 * rows * width * depth * blocks, bytes_accessed=40_000_000, transcendentals=rows * width
        ),
    )(tokens, expert_ids.T, combine.T, gate_q, gate_scale.T, up_q, up_scale.T, down_q, down_scale)


def solution(mesh):
    placed = (
        P(("groups", "dp"), "tensor"),
        P(("groups", "dp"), None),
        P(("groups", "dp"), None),
        P(("groups", "dp")),
        P("dp", "tensor"),
        P("dp", "tensor"),
        P("dp", "tensor"),
        P("dp", "tensor"),
        P("tensor", "dp"),
        P("tensor", "dp"),
    )
    sizes = tuple(mesh.shape[a] for a in ("groups", "dp", "tensor"))
    body = functools.partial(pair_body, nx=2, nz=4) if sizes == (2, 8, 2) else general_body
    return jax.shard_map(
        body, mesh=mesh, in_specs=placed, out_specs=P(("groups", "dp"), "tensor"), check_vma=False
    )
```

```python
import functools

import jax
import jax.numpy as jnp
from jax import lax
from jax.experimental import pallas as pl
from jax.experimental.pallas import tpu as pltpu
from jax.sharding import PartitionSpec as P

MESH = pl.DeviceIdType.MESH
F32 = jnp.float32
BF16 = jnp.bfloat16


def dequantize(values, scales, tile_axis):
    tile_len = values.shape[tile_axis] // scales.shape[tile_axis]
    return (values.astype(F32) * jnp.repeat(scales, tile_len, axis=tile_axis)).astype(BF16)


def general_body(
    tokens, expert_ids, combine, row_list, gate_q, gate_scale, up_q, up_scale, down_q, down_scale
):
    del row_list
    full_tokens = lax.all_gather(tokens, "tensor", axis=1, tiled=True)
    row_weight = jnp.sum(jnp.where(expert_ids == 0, combine, 0.0), axis=1)
    gate_w = lax.all_gather(dequantize(gate_q, gate_scale, 1), "dp", axis=0, tiled=True)
    up_w = lax.all_gather(dequantize(up_q, up_scale, 1), "dp", axis=0, tiled=True)
    down_w = lax.all_gather(dequantize(down_q, down_scale, 0), "dp", axis=1, tiled=True)
    gate_act = jnp.dot(full_tokens, gate_w, preferred_element_type=F32)
    up_act = jnp.dot(full_tokens, up_w, preferred_element_type=F32)
    hidden = (jax.nn.silu(gate_act) * up_act).astype(BF16)
    part = jnp.dot(hidden, down_w, preferred_element_type=F32) * row_weight[:, None]
    return lax.psum_scatter(part.astype(BF16), "tensor", scatter_dimension=1, tiled=True)


def kernel(
    nx, nz,
    tok, ids_h, comb_h, gq_h, gs_h, uq_h, us_h, dq_h, ds_h,
    out,
    gs, gq, us, uq, ds, dq, ids, comb, in_sem, T, W, D, wt, acc, ps, pr, hid, o_own, o_send, o_recv,
    st_send, st_recv, f_send, f_recv, sl, w_send, wx_send, w_recv, d_send, dx_send, dy_send, d_recv,
    p_send, p_recv, q_send, q_recv,
):
    y = lax.axis_index("groups")
    dp = lax.axis_index("dp")
    t = lax.axis_index("tensor")
    z, x = dp // nx, dp % nx
    oy, ot, ox = 1 - y, 1 - t, 1 - x
    rows = out.shape[0]
    win = W.shape[2]
    depth, width = gq.shape
    half = depth // 2
    pad = win - half
    real = pl.ds(pl.multiple_of(y * pad, pad), half)
    zero = pl.ds(pl.multiple_of((1 - y) * half, pad), pad)
    hd = D.shape[2]
    blk = D.shape[3]
    per_core = nx * nz // 2
    up_ok, down_ok = z < nz - 1, z > 0
    ydev, tdev, xdev = (oy, dp, t), (y, dp, ot), (y, z * nx + ox, t)
    zdev = ((y, dp + nx, t), (y, dp - nx, t))
    zok = (up_ok, down_ok)

    sources = (gs_h, gq_h, us_h, uq_h, ds_h, dq_h, ids_h, comb_h)
    targets = (gs, gq, us, uq, ds, dq, ids, comb)
    loads = [pltpu.make_async_copy(a, b, in_sem.at[i]) for i, (a, b) in enumerate(zip(sources, targets))]
    for load in loads:
        load.start()

    barrier = pltpu.get_barrier_semaphore()
    for dev in (ydev, tdev, xdev):
        pl.semaphore_signal(barrier, inc=1, device_id=dev, device_id_type=MESH)
    for k in range(2):
        @pl.when(zok[k])
        def _():
            pl.semaphore_signal(barrier, inc=1, device_id=zdev[k], device_id_type=MESH)

    def remote(src, dst, s, r, dev):
        return pltpu.make_async_remote_copy(
            src_ref=src, dst_ref=dst, send_sem=s, recv_sem=r, device_id=dev, device_id_type=MESH
        )

    def feats(j, v):
        return tok.at[:, pl.ds(pl.multiple_of(j * depth + v * (depth - win), 128), win)]

    def slot(side, who, j):
        return T.at[side, who, :, pl.ds(j * win, win)]

    def own_tok(j):
        return pltpu.make_async_copy(feats(j, y), slot(0, 0, j), sl.at[j])

    def tok_y(j):
        return remote(feats(j, oy), slot(0, 1, j), st_send.at[0, j], st_recv.at[0, j], ydev)

    def tok_t(j):
        return remote(feats(j, y), slot(1, 0, j), st_send.at[1, j], st_recv.at[1, j], tdev)

    tok_f = remote(T.at[0, 1], T.at[1, 1], f_send, f_recv, tdev)
    for j in range(per_core):
        own_tok(j).start()

    cut = width - width % 256 if width % 256 else width // 2
    pieces = ((0, 0, width), (1, 0, cut), (1, cut, width - cut))

    def wref(m, b):
        i, lo, n = pieces[m]
        return W.at[i, b, real, pl.ds(lo, n)]

    def wz(m, k, s):
        b = (z - s if k == 0 else z + s) * nx + x
        ref = wref(m, b)
        return remote(ref, ref, w_send.at[m, k, s], w_recv.at[m, b], zdev[k])

    def wx(m, zz):
        b = zz * nx + x
        ref = wref(m, b)
        return remote(ref, ref, wx_send.at[m, zz], w_recv.at[m, b], xdev)

    def w_wait(m, b):
        ref = wref(m, b)
        remote(ref, ref, wx_send.at[m, 0], w_recv.at[m, b], xdev).wait_recv()

    def dz(q, k, s):
        b = (z - s if k == 0 else z + s) * nx + x
        return remote(D.at[b, q], D.at[b, q], d_send.at[q, k, s], d_recv.at[b, q], zdev[k])

    def dx(zz, i):
        b, q = zz * nx + x, 2 * y + i
        return remote(D.at[b, q], D.at[b, q], dx_send.at[zz, i], d_recv.at[b, q], xdev)

    def dy(zz, i):
        b, q = zz * nx + ox, 2 * y + i
        return remote(D.at[b, q], D.at[b, q], dy_send.at[zz, i], d_recv.at[b, q], ydev)

    def d_wait(b, q):
        remote(D.at[b, q], D.at[b, q], dx_send.at[0, 0], d_recv.at[b, q], xdev).wait_recv()

    def spread(row):
        return jnp.broadcast_to(row, (128, row.shape[1])).T

    def scale_block(m, q, s):
        first = pl.multiple_of(y * (depth - win), 128)
        for j in range(s.shape[0]):
            cols = pl.ds(j * 128, 128)
            v = q[pl.ds(first, win), cols].astype(F32)
            W[m, dp, :, cols] = (v * spread(s[j : j + 1, pl.ds(first, win)])).astype(BF16)

    loads[0].wait()
    loads[1].wait()
    scale_block(0, gq, gs)
    pl.semaphore_wait(barrier, 3 + jnp.where(up_ok, 1, 0) + jnp.where(down_ok, 1, 0))

    def start_own_w(m, along_x=True):
        for k in range(2):
            @pl.when(zok[k])
            def _():
                wz(m, k, 0).start()
        if along_x:
            wx(m, z).start()

    start_own_w(0)
    for j in range(per_core):
        tok_y(j).start()
        tok_t(j).start()
    loads[2].wait()
    loads[3].wait()
    scale_block(1, uq, us)
    start_own_w(1)
    loads[4].wait()
    loads[5].wait()
    for j in range(ds.shape[0]):
        lo = j * 128
        v = (dq[lo : lo + 128, :].astype(F32) * ds[j : j + 1, :]).astype(BF16)
        while lo < (j + 1) * 128:
            n = min((j + 1) * 128, (lo // hd + 1) * hd) - lo
            D[dp, lo // hd, lo % hd : lo % hd + n, :] = v[lo - j * 128 : lo - j * 128 + n]
            lo += n

    def each_arrival(s, body):
        if s >= nz:
            return

        @pl.when(z - s >= 0)
        def _():
            body(z - s, 0)

        @pl.when(z + s < nz)
        def _():
            body(z + s, 1)

    def w_event(m, s):
        def body(zz, k):
            w_wait(m, zz * nx + x)

            @pl.when(zok[k])
            def _():
                wz(m, k, s).start()

            wx(m, zz).start()

        each_arrival(s, body)

    def start_own_d(h):
        for i in range(2):
            for k in range(2):
                @pl.when(zok[k])
                def _():
                    dz(2 * h + i, k, 0).start()

    def d_event(h, s, cross):
        def body(zz, k):
            for i in range(2):
                d_wait(zz * nx + x, 2 * h + i)

                @pl.when(zok[k])
                def _():
                    dz(2 * h + i, k, s).start()

                if cross:
                    dx(zz, i).start()

        each_arrival(s, body)

    def dy_event(s):
        def body(zz, k):
            for i in range(2):
                d_wait(zz * nx + ox, 2 * y + i)
                dy(zz, i).start()

        if s == 0:
            body(z, 0)
        else:
            each_arrival(s, body)

    tile = 192

    def partial_act(m):
        mat, lo, n = pieces[m]
        cols = pl.ds(lo, n)
        for zz in range(nz):
            w_wait(m, zz * nx + ox)
        for who in (1, 0):
            @pl.loop(0, rows // tile)
            def _(i):
                r = pl.ds(pl.multiple_of(i * tile, tile), tile)
                total = None
                for side in range(2):
                    blocks = pl.ds((t if side == 0 else ot) * per_core, per_core)
                    w = W[mat, blocks, :, cols].reshape(per_core * win, n)
                    p = jnp.dot(T[side, who, r, :], w, preferred_element_type=F32)
                    total = p if total is None else total + p
                if who == 1:
                    ps[mat, r, cols] = total.astype(BF16)
                else:
                    acc[mat, r, cols] = total
            if who == 1:
                pcopy(m).start()

    def pcopy(m):
        mat, lo, n = pieces[m]
        cols = pl.ds(lo, n)
        return remote(ps.at[mat, :, cols], pr.at[mat, :, cols], p_send.at[m], p_recv.at[m], ydev)

    for m in range(2):
        @pl.loop(0, nx * nz)
        def _(b):
            W[m, b, zero] = jnp.zeros((pad, W.shape[3]), BF16)
    loads[6].wait()
    loads[7].wait()
    wt[...] = spread(jnp.sum(jnp.where(ids[...] == 0, comb[...], 0.0), axis=0, keepdims=True))

    w_event(0, 1)
    w_event(0, 2)
    start_own_d(y)
    start_own_w(2, along_x=False)
    w_event(0, 3)
    for i in range(2):
        dx(z, i).start()
    w_event(1, 1)
    for j in range(per_core):
        tok_y(j).wait_recv()
    tok_f.start()
    for j in range(per_core):
        own_tok(j).wait()
        tok_t(j).wait_recv()
    d_event(y, 1, True)
    w_event(1, 2)
    tok_f.wait_recv()
    partial_act(0)
    dy_event(0)
    w_event(1, 3)
    wx(2, z).start()
    for s in range(1, nz):
        w_event(2, s)
    d_event(y, 2, True)
    dy_event(1)
    start_own_d(oy)
    partial_act(1)
    d_event(y, 3, True)
    d_event(oy, 1, False)
    partial_act(2)
    dy_event(2)
    d_event(oy, 2, False)
    for m in range(len(pieces)):
        pcopy(m).wait_recv()
    for i in range(rows // tile):
        r = slice(i * tile, (i + 1) * tile)
        g = acc[0, r, :] + pr[0, r, :].astype(F32)
        u = acc[1, r, :] + pr[1, r, :].astype(F32)
        hid[r, :] = (g / (1.0 + jnp.exp(-g)) * u).astype(BF16)

    def qcopy(c):
        return remote(o_send.at[c], o_recv.at[c], q_send.at[c], q_recv.at[c], tdev)

    def down_block(b):
        c = b % per_core
        mine = b // per_core == t
        w = D[b].reshape(D.shape[1] * hd, blk)
        p = jnp.dot(hid[...], w, preferred_element_type=F32)
        p = [(p[:, i : i + 128] * wt[...]).astype(BF16) for i in range(0, blk, 128)]

        @pl.when(mine)
        def _():
            for i, v in enumerate(p):
                o_own[c, :, i * 128 : (i + 1) * 128] = v

        @pl.when(jnp.logical_not(mine))
        def _():
            for i, v in enumerate(p):
                o_send[c, :, i * 128 : (i + 1) * 128] = v
            qcopy(c).start()

    def nearest(k):
        low = jnp.where(k <= z, z - k, k)
        high = jnp.where(k <= nz - 1 - z, z + k, nz - 1 - k)
        return jnp.where(2 * z < nz, low, high)

    dy_event(3)
    d_event(oy, 3, False)

    def add_blocks(col):
        for i in range(per_core // nx):
            c = i * nx + col
            qcopy(c).wait_recv()
            total = o_own[c].astype(F32) + o_recv[c].astype(F32)
            out[:, pl.ds(pl.multiple_of(c * blk, 128), blk)] = total.astype(BF16)

    @pl.loop(0, nz)
    def _(k):
        down_block(nearest(k) * nx + x)

    add_blocks(x)

    @pl.loop(0, nz)
    def _(k):
        zz = nearest(k)
        for i in range(2):
            d_wait(zz * nx + ox, 2 * oy + i)
        down_block(zz * nx + ox)

    add_blocks(ox)

    for j in range(per_core):
        tok_y(j).wait_send()
        tok_t(j).wait_send()
    tok_f.wait_send()
    for k in range(2):
        for s in range(nz - 1):
            here = (z - s >= 0) if k == 0 else (z + s < nz)

            @pl.when(jnp.logical_and(here, zok[k]))
            def _():
                for m in range(len(pieces)):
                    wz(m, k, s).wait_send()
                for q in range(4):
                    dz(q, k, s).wait_send()
    for zz in range(nz):
        for m in range(len(pieces)):
            wx(m, zz).wait_send()
        for i in range(2):
            dx(zz, i).wait_send()
            dy(zz, i).wait_send()
    for m in range(len(pieces)):
        pcopy(m).wait_send()
    for c in range(per_core):
        qcopy(c).wait_send()


def pair_body(
    tokens, expert_ids, combine, row_list, gate_q, gate_scale, up_q, up_scale, down_q, down_scale,
    *, nx, nz
):
    del row_list
    rows, feats = tokens.shape
    depth, width = gate_q.shape
    win = -(-(depth // 2) // 128) * 128
    blocks = nx * nz
    per_core = blocks // 2
    hd = down_q.shape[0] // 4
    blk = down_q.shape[1]
    vmem = pl.BlockSpec(memory_space=pltpu.VMEM)
    dma = pltpu.SemaphoreType.DMA
    return pl.pallas_call(
        functools.partial(kernel, nx, nz),
        out_shape=jax.ShapeDtypeStruct((rows, feats), BF16),
        in_specs=[pl.BlockSpec(memory_space=pltpu.HBM)] * 9,
        out_specs=vmem,
        scratch_shapes=[
            pltpu.VMEM(gate_scale.shape[::-1], F32),
            pltpu.VMEM(gate_q.shape, BF16),
            pltpu.VMEM(up_scale.shape[::-1], F32),
            pltpu.VMEM(up_q.shape, BF16),
            pltpu.VMEM(down_scale.shape, F32),
            pltpu.VMEM(down_q.shape, BF16),
            pltpu.VMEM(expert_ids.shape[::-1], jnp.int32),
            pltpu.VMEM(combine.shape[::-1], F32),
            dma((8,)),
            pltpu.VMEM((2, 2, rows, per_core * win), BF16),
            pltpu.VMEM((2, blocks, win, width), BF16),
            pltpu.VMEM((blocks, 4, hd, blk), BF16),
            pltpu.VMEM((rows, 128), F32),
            pltpu.VMEM((2, rows, width), F32),
            pltpu.VMEM((2, rows, width), BF16),
            pltpu.VMEM((2, rows, width), BF16),
            pltpu.VMEM((rows, width), BF16),
            pltpu.VMEM((per_core, rows, blk), BF16),
            pltpu.VMEM((per_core, rows, blk), BF16),
            pltpu.VMEM((per_core, rows, blk), BF16),
            dma((2, per_core)), dma((2, per_core)), dma, dma, dma((per_core,)),
            dma((3, 2, nz)), dma((3, nz)), dma((3, blocks)),
            dma((4, 2, nz)), dma((nz, 2)), dma((nz, 2)), dma((blocks, 4)),
            dma((3,)), dma((3,)), dma((per_core,)), dma((per_core,)),
        ],
        compiler_params=pltpu.CompilerParams(
            collective_id=0, has_side_effects=True, vmem_limit_bytes=56 * 1024 * 1024
        ),
        cost_estimate=pl.CostEstimate(
            flops=6 * rows * width * depth * blocks, bytes_accessed=40_000_000, transcendentals=rows * width
        ),
    )(tokens, expert_ids.T, combine.T, gate_q, gate_scale.T, up_q, up_scale.T, down_q, down_scale)


def solution(mesh):
    placed = (
        P(("groups", "dp"), "tensor"),
        P(("groups", "dp"), None),
        P(("groups", "dp"), None),
        P(("groups", "dp")),
        P("dp", "tensor"),
        P("dp", "tensor"),
        P("dp", "tensor"),
        P("dp", "tensor"),
        P("tensor", "dp"),
        P("tensor", "dp"),
    )
    sizes = tuple(mesh.shape[a] for a in ("groups", "dp", "tensor"))
    body = functools.partial(pair_body, nx=2, nz=4) if sizes == (2, 8, 2) else general_body
    return jax.shard_map(
        body, mesh=mesh, in_specs=placed, out_specs=P(("groups", "dp"), "tensor"), check_vma=False
    )
```

```python
import functools

import jax
import jax.numpy as jnp
from jax import lax
from jax.experimental import pallas as pl
from jax.experimental.pallas import tpu as pltpu
from jax.sharding import PartitionSpec as P

MESH = pl.DeviceIdType.MESH
F32 = jnp.float32
BF16 = jnp.bfloat16


def dequantize(values, scales, tile_axis):
    tile_len = values.shape[tile_axis] // scales.shape[tile_axis]
    return (values.astype(F32) * jnp.repeat(scales, tile_len, axis=tile_axis)).astype(BF16)


def general_body(
    tokens, expert_ids, combine, row_list, gate_q, gate_scale, up_q, up_scale, down_q, down_scale
):
    del row_list
    full_tokens = lax.all_gather(tokens, "tensor", axis=1, tiled=True)
    row_weight = jnp.sum(jnp.where(expert_ids == 0, combine, 0.0), axis=1)
    gate_w = lax.all_gather(dequantize(gate_q, gate_scale, 1), "dp", axis=0, tiled=True)
    up_w = lax.all_gather(dequantize(up_q, up_scale, 1), "dp", axis=0, tiled=True)
    down_w = lax.all_gather(dequantize(down_q, down_scale, 0), "dp", axis=1, tiled=True)
    gate_act = jnp.dot(full_tokens, gate_w, preferred_element_type=F32)
    up_act = jnp.dot(full_tokens, up_w, preferred_element_type=F32)
    hidden = (jax.nn.silu(gate_act) * up_act).astype(BF16)
    part = jnp.dot(hidden, down_w, preferred_element_type=F32) * row_weight[:, None]
    return lax.psum_scatter(part.astype(BF16), "tensor", scatter_dimension=1, tiled=True)


def kernel(
    nx, nz,
    tok, ids_h, comb_h, gq_h, gs_h, uq_h, us_h, dq_h, ds_h,
    out,
    gs, gq, us, uq, ds, dq, ids, comb, in_sem, T, W, D, wt, acc, ps, pr, hid, o_own, o_send, o_recv,
    st_send, st_recv, f_send, f_recv, sl, w_send, wx_send, w_recv, d_send, dx_send, dy_send, d_recv,
    p_send, p_recv, q_send, q_recv,
):
    y = lax.axis_index("groups")
    dp = lax.axis_index("dp")
    t = lax.axis_index("tensor")
    z, x = dp // nx, dp % nx
    oy, ot, ox = 1 - y, 1 - t, 1 - x
    rows = out.shape[0]
    win = W.shape[2]
    depth = gq.shape[0]
    half = depth // 2
    pad = win - half
    real = pl.ds(pl.multiple_of(y * pad, pad), half)
    zero = pl.ds(pl.multiple_of((1 - y) * half, pad), pad)
    hd = D.shape[2]
    blk = D.shape[3]
    per_core = nx * nz // 2
    up_ok, down_ok = z < nz - 1, z > 0
    ydev, tdev, xdev = (oy, dp, t), (y, dp, ot), (y, z * nx + ox, t)
    zdev = ((y, dp + nx, t), (y, dp - nx, t))
    zok = (up_ok, down_ok)

    sources = (gs_h, gq_h, us_h, uq_h, ds_h, dq_h, ids_h, comb_h)
    targets = (gs, gq, us, uq, ds, dq, ids, comb)
    loads = [pltpu.make_async_copy(a, b, in_sem.at[i]) for i, (a, b) in enumerate(zip(sources, targets))]
    for load in loads:
        load.start()

    barrier = pltpu.get_barrier_semaphore()
    for dev in (ydev, tdev, xdev):
        pl.semaphore_signal(barrier, inc=1, device_id=dev, device_id_type=MESH)
    for k in range(2):
        @pl.when(zok[k])
        def _():
            pl.semaphore_signal(barrier, inc=1, device_id=zdev[k], device_id_type=MESH)

    def remote(src, dst, s, r, dev):
        return pltpu.make_async_remote_copy(
            src_ref=src, dst_ref=dst, send_sem=s, recv_sem=r, device_id=dev, device_id_type=MESH
        )

    def feats(j, v):
        return tok.at[:, pl.ds(pl.multiple_of(j * depth + v * (depth - win), 128), win)]

    def slot(side, who, j):
        return T.at[side, who, :, pl.ds(j * win, win)]

    def own_tok(j):
        return pltpu.make_async_copy(feats(j, y), slot(0, 0, j), sl.at[j])

    def tok_y(j):
        return remote(feats(j, oy), slot(0, 1, j), st_send.at[0, j], st_recv.at[0, j], ydev)

    def tok_t(j):
        return remote(feats(j, y), slot(1, 0, j), st_send.at[1, j], st_recv.at[1, j], tdev)

    tok_f = remote(T.at[0, 1], T.at[1, 1], f_send, f_recv, tdev)
    for j in range(per_core):
        own_tok(j).start()

    def wz(m, k, s):
        b = (z - s if k == 0 else z + s) * nx + x
        ref = W.at[m, b, real]
        return remote(ref, ref, w_send.at[m, k, s], w_recv.at[m, b], zdev[k])

    def wx(m, zz):
        b = zz * nx + x
        ref = W.at[m, b, real]
        return remote(ref, ref, wx_send.at[m, zz], w_recv.at[m, b], xdev)

    def w_wait(m, b):
        ref = W.at[m, b, real]
        remote(ref, ref, wx_send.at[m, 0], w_recv.at[m, b], xdev).wait_recv()

    def dz(h, k, s):
        b = (z - s if k == 0 else z + s) * nx + x
        return remote(D.at[b, h], D.at[b, h], d_send.at[h, k, s], d_recv.at[b, h], zdev[k])

    def dx(zz):
        b = zz * nx + x
        return remote(D.at[b, y], D.at[b, y], dx_send.at[zz], d_recv.at[b, y], xdev)

    def dy(zz):
        b = zz * nx + ox
        return remote(D.at[b, y], D.at[b, y], dy_send.at[zz], d_recv.at[b, y], ydev)

    def d_wait(b, h):
        remote(D.at[b, h], D.at[b, h], dx_send.at[0], d_recv.at[b, h], xdev).wait_recv()

    def spread(row):
        return jnp.broadcast_to(row, (128, row.shape[1])).T

    def scale_block(m, q, s):
        first = pl.multiple_of(y * (depth - win), 128)
        for j in range(s.shape[0]):
            cols = pl.ds(j * 128, 128)
            v = q[pl.ds(first, win), cols].astype(F32)
            W[m, dp, :, cols] = (v * spread(s[j : j + 1, pl.ds(first, win)])).astype(BF16)

    loads[0].wait()
    loads[1].wait()
    scale_block(0, gq, gs)
    pl.semaphore_wait(barrier, 3 + jnp.where(up_ok, 1, 0) + jnp.where(down_ok, 1, 0))

    def start_own_w(m):
        for k in range(2):
            @pl.when(zok[k])
            def _():
                wz(m, k, 0).start()
        wx(m, z).start()

    start_own_w(0)
    for j in range(per_core):
        tok_y(j).start()
        tok_t(j).start()
    loads[2].wait()
    loads[3].wait()
    scale_block(1, uq, us)
    loads[4].wait()
    loads[5].wait()
    for j in range(ds.shape[0]):
        lo = j * 128
        v = (dq[lo : lo + 128, :].astype(F32) * ds[j : j + 1, :]).astype(BF16)
        while lo < (j + 1) * 128:
            n = min((j + 1) * 128, (lo // hd + 1) * hd) - lo
            D[dp, lo // hd, lo % hd : lo % hd + n, :] = v[lo - j * 128 : lo - j * 128 + n]
            lo += n

    def each_arrival(s, body):
        if s >= nz:
            return

        @pl.when(z - s >= 0)
        def _():
            body(z - s, 0)

        @pl.when(z + s < nz)
        def _():
            body(z + s, 1)

    def w_event(m, s):
        def body(zz, k):
            w_wait(m, zz * nx + x)

            @pl.when(zok[k])
            def _():
                wz(m, k, s).start()

            wx(m, zz).start()

        each_arrival(s, body)

    def start_own_d(h):
        for k in range(2):
            @pl.when(zok[k])
            def _():
                dz(h, k, 0).start()

    def d_event(h, s, cross):
        def body(zz, k):
            d_wait(zz * nx + x, h)

            @pl.when(zok[k])
            def _():
                dz(h, k, s).start()

            if cross:
                dx(zz).start()

        each_arrival(s, body)

    def dy_event(s):
        def body(zz, k):
            d_wait(zz * nx + ox, y)
            dy(zz).start()

        if s == 0:
            body(z, 0)
        else:
            each_arrival(s, body)

    tile = 192

    def partial_act(m):
        for zz in range(nz):
            w_wait(m, zz * nx + ox)
        for who in (1, 0):
            @pl.loop(0, rows // tile)
            def _(i):
                r = pl.ds(pl.multiple_of(i * tile, tile), tile)
                total = None
                for side in range(2):
                    blocks = pl.ds((t if side == 0 else ot) * per_core, per_core)
                    w = W[m, blocks].reshape(per_core * win, W.shape[3])
                    p = jnp.dot(T[side, who, r, :], w, preferred_element_type=F32)
                    total = p if total is None else total + p
                if who == 1:
                    ps[m, r, :] = total.astype(BF16)
                else:
                    acc[m, r, :] = total
            if who == 1:
                pcopy(m).start()

    def pcopy(m):
        return remote(ps.at[m], pr.at[m], p_send.at[m], p_recv.at[m], ydev)

    for m in range(2):
        @pl.loop(0, nx * nz)
        def _(b):
            W[m, b, zero] = jnp.zeros((pad, W.shape[3]), BF16)
    loads[6].wait()
    loads[7].wait()
    wt[...] = spread(jnp.sum(jnp.where(ids[...] == 0, comb[...], 0.0), axis=0, keepdims=True))

    w_event(0, 1)
    start_own_w(1)
    w_event(0, 2)
    start_own_d(y)
    w_event(0, 3)
    dx(z).start()
    w_event(1, 1)
    for j in range(per_core):
        tok_y(j).wait_recv()
    tok_f.start()
    for j in range(per_core):
        own_tok(j).wait()
        tok_t(j).wait_recv()
    d_event(y, 1, True)
    w_event(1, 2)
    tok_f.wait_recv()
    partial_act(0)
    dy_event(0)
    w_event(1, 3)
    d_event(y, 2, True)
    start_own_d(oy)
    dy_event(1)
    d_event(y, 3, True)
    d_event(oy, 1, False)
    partial_act(1)
    dy_event(2)
    d_event(oy, 2, False)
    for m in range(2):
        pcopy(m).wait_recv()
    for i in range(rows // tile):
        r = slice(i * tile, (i + 1) * tile)
        g = acc[0, r, :] + pr[0, r, :].astype(F32)
        u = acc[1, r, :] + pr[1, r, :].astype(F32)
        hid[r, :] = (g / (1.0 + jnp.exp(-g)) * u).astype(BF16)

    def qcopy(c):
        return remote(o_send.at[c], o_recv.at[c], q_send.at[c], q_recv.at[c], tdev)

    def down_block(b):
        c = b % per_core
        mine = b // per_core == t
        w = D[b].reshape(2 * hd, blk)
        p = jnp.dot(hid[...], w, preferred_element_type=F32)
        p = [(p[:, i : i + 128] * wt[...]).astype(BF16) for i in range(0, blk, 128)]

        @pl.when(mine)
        def _():
            for i, v in enumerate(p):
                o_own[c, :, i * 128 : (i + 1) * 128] = v

        @pl.when(jnp.logical_not(mine))
        def _():
            for i, v in enumerate(p):
                o_send[c, :, i * 128 : (i + 1) * 128] = v
            qcopy(c).start()

    def nearest(k):
        low = jnp.where(k <= z, z - k, k)
        high = jnp.where(k <= nz - 1 - z, z + k, nz - 1 - k)
        return jnp.where(2 * z < nz, low, high)

    dy_event(3)
    d_event(oy, 3, False)

    def add_blocks(col):
        for i in range(per_core // nx):
            c = i * nx + col
            qcopy(c).wait_recv()
            total = o_own[c].astype(F32) + o_recv[c].astype(F32)
            out[:, pl.ds(pl.multiple_of(c * blk, 128), blk)] = total.astype(BF16)

    @pl.loop(0, nz)
    def _(k):
        down_block(nearest(k) * nx + x)

    add_blocks(x)

    @pl.loop(0, nz)
    def _(k):
        zz = nearest(k)
        d_wait(zz * nx + ox, oy)
        down_block(zz * nx + ox)

    add_blocks(ox)

    for j in range(per_core):
        tok_y(j).wait_send()
        tok_t(j).wait_send()
    tok_f.wait_send()
    for k in range(2):
        for s in range(nz - 1):
            here = (z - s >= 0) if k == 0 else (z + s < nz)

            @pl.when(jnp.logical_and(here, zok[k]))
            def _():
                for m in range(2):
                    wz(m, k, s).wait_send()
                for h in range(2):
                    dz(h, k, s).wait_send()
    for zz in range(nz):
        for m in range(2):
            wx(m, zz).wait_send()
        dx(zz).wait_send()
        dy(zz).wait_send()
    for m in range(2):
        pcopy(m).wait_send()
    for c in range(per_core):
        qcopy(c).wait_send()


def pair_body(
    tokens, expert_ids, combine, row_list, gate_q, gate_scale, up_q, up_scale, down_q, down_scale,
    *, nx, nz
):
    del row_list
    rows, feats = tokens.shape
    depth, width = gate_q.shape
    win = -(-(depth // 2) // 128) * 128
    blocks = nx * nz
    per_core = blocks // 2
    hd = down_q.shape[0] // 2
    blk = down_q.shape[1]
    vmem = pl.BlockSpec(memory_space=pltpu.VMEM)
    dma = pltpu.SemaphoreType.DMA
    return pl.pallas_call(
        functools.partial(kernel, nx, nz),
        out_shape=jax.ShapeDtypeStruct((rows, feats), BF16),
        in_specs=[pl.BlockSpec(memory_space=pltpu.HBM)] * 9,
        out_specs=vmem,
        scratch_shapes=[
            pltpu.VMEM(gate_scale.shape[::-1], F32),
            pltpu.VMEM(gate_q.shape, BF16),
            pltpu.VMEM(up_scale.shape[::-1], F32),
            pltpu.VMEM(up_q.shape, BF16),
            pltpu.VMEM(down_scale.shape, F32),
            pltpu.VMEM(down_q.shape, BF16),
            pltpu.VMEM(expert_ids.shape[::-1], jnp.int32),
            pltpu.VMEM(combine.shape[::-1], F32),
            dma((8,)),
            pltpu.VMEM((2, 2, rows, per_core * win), BF16),
            pltpu.VMEM((2, blocks, win, width), BF16),
            pltpu.VMEM((blocks, 2, hd, blk), BF16),
            pltpu.VMEM((rows, 128), F32),
            pltpu.VMEM((2, rows, width), F32),
            pltpu.VMEM((2, rows, width), BF16),
            pltpu.VMEM((2, rows, width), BF16),
            pltpu.VMEM((rows, width), BF16),
            pltpu.VMEM((per_core, rows, blk), BF16),
            pltpu.VMEM((per_core, rows, blk), BF16),
            pltpu.VMEM((per_core, rows, blk), BF16),
            dma((2, per_core)), dma((2, per_core)), dma, dma, dma((per_core,)),
            dma((2, 2, nz)), dma((2, nz)), dma((2, blocks)),
            dma((2, 2, nz)), dma((nz,)), dma((nz,)), dma((blocks, 2)),
            dma((2,)), dma((2,)), dma((per_core,)), dma((per_core,)),
        ],
        compiler_params=pltpu.CompilerParams(
            collective_id=0, has_side_effects=True, vmem_limit_bytes=56 * 1024 * 1024
        ),
        cost_estimate=pl.CostEstimate(
            flops=6 * rows * width * depth * blocks, bytes_accessed=40_000_000, transcendentals=rows * width
        ),
    )(tokens, expert_ids.T, combine.T, gate_q, gate_scale.T, up_q, up_scale.T, down_q, down_scale)


def solution(mesh):
    placed = (
        P(("groups", "dp"), "tensor"),
        P(("groups", "dp"), None),
        P(("groups", "dp"), None),
        P(("groups", "dp")),
        P("dp", "tensor"),
        P("dp", "tensor"),
        P("dp", "tensor"),
        P("dp", "tensor"),
        P("tensor", "dp"),
        P("tensor", "dp"),
    )
    sizes = tuple(mesh.shape[a] for a in ("groups", "dp", "tensor"))
    body = functools.partial(pair_body, nx=2, nz=4) if sizes == (2, 8, 2) else general_body
    return jax.shard_map(
        body, mesh=mesh, in_specs=placed, out_specs=P(("groups", "dp"), "tensor"), check_vma=False
    )
```
